32 devices in a mesh: row: 4 (over x, core), col: 8 (over z, y).
Axes of the slice: x: 2, y: 2, z: 4, core: 2. Of those that a mesh axis runs over, the one named last changes fastest.
Arguments:
- factor_panel: bfloat16 [3584, 98304], P('row', 'col'), may hold values from -1 to 1, as said below
- normal_draws: bfloat16 [98304, 256], P('col'), may hold values from -6 to 6
- inter_event: float32 [256], replicated, may hold values from -2.5 to 2.5
- site_owner: int32 [3584], replicated, may hold values from 0 to 31, as said below
- asset_site: int32 [65536], P(('row', 'col')), may hold values from 0 to 3583, as said below
- asset_class: int32 [65536], P(('row', 'col')), may hold values from 0 to 127
- asset_value: bfloat16 [65536], P(('row', 'col')), may hold values from 0.19921875 to 5
- asset_count: int32 [32], P(('row', 'col')), may hold values from 512 to 2048, as said below
- damage_curve: bfloat16 [32, 128], replicated, may hold values from 0 to 1
Outputs:
- residuals: float32 [3584, 256], P(('row', 'col'))
- asset_loss: float32 [65536, 256], P(('row', 'col'))
- region_loss: float32 [8, 256], P('col')
The draws below stay inside these ranges and needn't reach their ends.
Inputs may be any that keep to these rules, and one draw needn't show every extreme that they name: `factor_panel`: row i is zero beyond column 94720 + i and holds 0.7 there. `site_owner`: each aligned block of 112 sites (block d for device d = row index * 8 + col index) names each owner at most 7 times; some owner is named 7 times in every block; every owner is named somewhere. `asset_site`: every asset of block d of 2048 slots lies at a site whose owner is d. `asset_count`: some block has all 2048 slots live.
All inputs are finite; a program needn't handle non-finite values.
Results may differ from the reference program's by a relative error of at most 0.0037.
Values may be sent and summed in bfloat16 or wider, within the bound.
A program may use at most 128 MiB of HBM per device.

```python
import math
import jax
import jax.numpy as jnp
import numpy as np
from jax import lax

NS = 98304
EV = 256
K = 32
C = 128
SITES_DEV = 112
A_DEV = 2048
NW = 3584
ASSETS = 65536
CAP = 7
BUSIEST_OWNERS = 4
N_ROW = 4
N_COL = 8
DEVICES = 32


def owner_table(key):
    hot_key = jax.random.fold_in(key, 101)
    cover_key = jax.random.fold_in(key, 102)
    noise_key = jax.random.fold_in(key, 103)
    shuffle_key = jax.random.fold_in(key, 104)
    busiest_rank = jax.random.permutation(hot_key, DEVICES)
    coverage_flags = jax.random.permutation(cover_key, DEVICES)
    slot_span_width = DEVICES * CAP
    slot_position = jnp.arange(slot_span_width, dtype=jnp.int32)
    slot_holder = slot_position // CAP
    random_jitter = jax.random.randint(noise_key, (DEVICES, slot_span_width), 0, 1024, dtype=jnp.int32)
    extra_busiest = jnp.where(busiest_rank[slot_holder] < BUSIEST_OWNERS, 4096, 0).astype(jnp.int32)
    leading_slot = slot_position % CAP == 0
    extra_coverage = jnp.where((slot_holder[None, :] == coverage_flags[:, None]) & leading_slot[None, :], 2048, 0).astype(jnp.int32)
    ranking_scores = (random_jitter + extra_busiest[None, :] + extra_coverage) * slot_span_width + slot_position[None, :]
    picked = lax.top_k(ranking_scores, SITES_DEV)[1]
    owners = (picked // CAP).astype(jnp.int32)
    shuffle_scores = jax.random.randint(shuffle_key, (DEVICES, SITES_DEV), 0, 1 << 20, dtype=jnp.int32) * SITES_DEV + jnp.arange(SITES_DEV, dtype=jnp.int32)[None, :]
    order = jnp.argsort(shuffle_scores, axis=1)
    owners = jnp.take_along_axis(owners, order, axis=1)
    return owners.reshape(NW).astype(jnp.int32)


def draw_site_owner(key, part):
    return owner_table(key)


def draw_asset_site(key, part):
    owners = owner_table(key)
    order_sites = jnp.argsort(owners, stable=True).astype(jnp.int32)
    counts = jnp.sum((owners[None, :] == jnp.arange(DEVICES, dtype=jnp.int32)[:, None]).astype(jnp.int32), axis=1)
    starts = jnp.cumsum(counts) - counts
    pick_key = jax.random.fold_in(key, 105)
    chosen = jax.random.randint(pick_key, (DEVICES, A_DEV), 0, 1 << 24, dtype=jnp.int32) % counts[:, None] + starts[:, None]
    return order_sites[chosen].reshape(ASSETS).astype(jnp.int32)


def draw_asset_count(key, part):
    count_key = jax.random.fold_in(key, 201)
    full_key = jax.random.fold_in(key, 202)
    counts = jax.random.randint(count_key, (DEVICES,), A_DEV // 4, A_DEV + 1, dtype=jnp.int32)
    full_dev = jax.random.randint(full_key, (), 0, DEVICES, dtype=jnp.int32)
    return jnp.where(jnp.arange(DEVICES, dtype=jnp.int32) == full_dev, A_DEV, counts).astype(jnp.int32)


def draw_factor_panel(key, part):
    row_pos = lax.broadcasted_iota(jnp.int32, (NW, NS), 0)
    col_pos = lax.broadcasted_iota(jnp.int32, (NW, NS), 1)
    diag_col = NS - NW + row_pos
    base = jax.random.truncated_normal(key, -6.0, 6.0, (NW, NS), jnp.float32) * (0.5 / NS) ** 0.5
    entries = jnp.where(col_pos < diag_col, base, 0.0) + jnp.where(col_pos == diag_col, 0.7, 0.0)
    return entries.astype(jnp.bfloat16)


def draw_damage_curve(key, part):
    middle_key = jax.random.fold_in(key, 301)
    width_key = jax.random.fold_in(key, 302)
    noise_key = jax.random.fold_in(key, 303)
    middle = jax.random.uniform(middle_key, (1, C), jnp.float32, 0.2 * K, 0.8 * K)
    spread = jax.random.uniform(width_key, (1, C), jnp.float32, 1.0, K / 4.0)
    random_jitter = jax.random.uniform(noise_key, (K, C), jnp.float32, 0.8, 1.2)
    grid = lax.broadcasted_iota(jnp.float32, (K, C), 0)
    curve = 0.75 * random_jitter / (1.0 + jnp.exp(-(grid - middle) / spread))
    return curve.astype(jnp.bfloat16)


def place_ends(result, rng, low, top_value):
    dims = result.shape
    place = [jax.random.randint(jax.random.fold_in(rng, axis), (), 0, dims[axis]) for axis in range(len(dims))]
    result = result.at[tuple(place)].set(low)
    longest = dims.index(max(dims))
    place[longest] = (place[longest] + 1) % dims[longest]
    return result.at[tuple(place)].set(top_value)


def levels(stream_key, extent, pieces, least, top_value):
    level, own = 1.0, jax.random.fold_in(stream_key, 6)
    for dim, shards_of in pieces:
        heights = jnp.exp(jax.random.uniform(jax.random.fold_in(own, dim), (shards_of,), jnp.float32, least / len(pieces), top_value / len(pieces)))
        level = level * jnp.repeat(heights, extent[dim] // shards_of).reshape([-1 if axis == dim else 1 for axis in range(len(extent))])
    return level


def rank_table(number_of, lean):
    weights = [(1 << 20) // math.isqrt(grade ** lean) + 1 for grade in range(1, number_of + 1)]
    deviation = 1 + sum(weights) // (1 << 30)
    return np.cumsum(np.array([max(1, weight // deviation) for weight in weights]))


def ranked_ids(rng, dims, count, lean):
    listing = rank_table(count, lean)
    lot = jax.random.randint(jax.random.fold_in(rng, 1), dims, 0, int(listing[count - 1]))
    grade = jnp.searchsorted(jnp.asarray(listing, jnp.int32), lot, side="right")
    return jax.random.permutation(jax.random.fold_in(rng, 2), count)[grade].astype(jnp.int32)


def bell_draw(key, extent, width, bound, cuts=(), kind=jnp.bfloat16):
    loudness = levels(key, extent, cuts, -0.22, 0.18) if cuts else 1.0
    drawn = jax.random.normal(key, extent, jnp.float32) * width * loudness
    return jnp.minimum(jnp.maximum(drawn, -bound), bound).astype(kind)


def setup_inputs(seed: int = 0) -> dict:
    streams_of = jax.random.split(jax.random.key(seed), 10)
    factor_panel = draw_factor_panel(jax.random.fold_in(streams_of[9], 71), 0)
    normal_draws = bell_draw(streams_of[1], (NS, EV), 1.0, 6.0, ((0, 8),))
    inter_event = bell_draw(streams_of[2], (EV,), 0.4, 2.5, (), jnp.float32)
    site_owner = draw_site_owner(jax.random.fold_in(streams_of[9], 71), 0)
    asset_site = draw_asset_site(jax.random.fold_in(streams_of[9], 71), 0)
    asset_class = place_ends(ranked_ids(streams_of[5], (ASSETS,), C, 2), jax.random.fold_in(streams_of[5], 3), 0, C - 1).astype(jnp.int32)
    asset_value = jnp.clip(jnp.exp(math.log(5.0) - 3.2227897 * jax.random.uniform(streams_of[6], (ASSETS,), jnp.float32) ** levels(streams_of[6], (ASSETS,), ((0, 32),), -0.2, 0.2)), 0.19921875, 5.0).astype(jnp.bfloat16)
    asset_count = draw_asset_count(jax.random.fold_in(streams_of[9], 71), 0)
    damage_curve = draw_damage_curve(jax.random.fold_in(streams_of[9], 71), 0)
    return {"factor_panel": factor_panel, "normal_draws": normal_draws, "inter_event": inter_event, "site_owner": site_owner, "asset_site": asset_site, "asset_class": asset_class, "asset_value": asset_value, "asset_count": asset_count, "damage_curve": damage_curve}


median_log = -1.0
intra_scale = 0.6
grid_low = -4.0
grid_span = 6.0


def reference(factor_panel, normal_draws, inter_event, site_owner, asset_site, asset_class, asset_value, asset_count, damage_curve):
    residual = jnp.dot(factor_panel, normal_draws, preferred_element_type=jnp.float32)
    log_motion = (median_log + intra_scale * residual + inter_event[None, :]).astype(jnp.bfloat16)
    asset_motion = log_motion[asset_site].astype(jnp.float32)
    curve_rows = damage_curve.astype(jnp.float32)[:, asset_class]
    level_pos = jnp.clip((asset_motion - grid_low) * ((K - 1) / grid_span), 0.0, K - 1.0)
    damage = jnp.zeros(level_pos.shape, jnp.float32)
    for level_idx in range(K):
        weights = jnp.maximum(0.0, 1.0 - jnp.abs(level_pos - level_idx))
        damage = damage + curve_rows[level_idx][:, None] * weights
    slot_index = jnp.arange(ASSETS, dtype=jnp.int32)
    block_index = (slot_index // A_DEV).astype(jnp.int32)
    owner_match = site_owner[asset_site].astype(jnp.int32) == block_index
    live_mask = (((slot_index % A_DEV) < asset_count[block_index]) & owner_match).astype(jnp.float32)
    asset_loss = asset_value.astype(jnp.float32)[:, None] * damage * live_mask[:, None]
    region_loss = jnp.sum(asset_loss.reshape(N_ROW, N_COL, A_DEV, EV), axis=(0, 2)) / (A_DEV * N_ROW)
    return residual, asset_loss, region_loss
```

```python
import functools

import jax
import jax.numpy as jnp
from jax import lax
from jax.experimental import pallas as pl
from jax.experimental.pallas import tpu as pltpu
from jax.sharding import PartitionSpec as P

median_log = -1.0
intra_scale = 0.6
grid_low = -4.0
grid_span = 6.0
SLOT = 8
TILE = 256
K1 = 60 * 1024
K2 = 60
PARTS = 8
WINDOW = 4
PAIRED = True
MESH = pl.DeviceIdType.MESH


def block_order(groups):
    ahead = min(3, groups - 1)
    order = [("A", g) for g in range(ahead)]
    order.append(("B", 0))
    for g in range(ahead, groups):
        order += [("B", g - ahead + 1), ("A", g)]
    return order + [("B", g) for g in range(groups - ahead + 1, groups)]


def earlier_mask(size):
    i = lax.broadcasted_iota(jnp.int32, (size, size), 0)
    j = lax.broadcasted_iota(jnp.int32, (size, size), 1)
    return (i < j).astype(jnp.float32).astype(jnp.bfloat16)


def motion_kernel(
    rows, cols,
    count_hbm, factor, draws, inter_hbm, owner_hbm, site_hbm, class_hbm, value_hbm, curve_hbm,
    res_out, loss_out, region_out,
    res_ref, loss_ref, region_ref, select_ref, table_ref, stage_ref, fbuf, dbuf, ysend, yrecv, held, zsend, zrecv, placing, outbuf, inbuf, regions, agg_ref, owner,
    count_ref, inter, flat, site_ref, class_ref, value_ref, curve_ref,
    fsem, dsem, yssem, yrsem, zssem, zrsem, ssem, rsem, gssem, grsem, smallsem, outsem,
):
    devices = rows * cols
    groups = cols // 2
    sites, depth = factor.shape[0] // cols, factor.shape[1]
    events = draws.shape[1]
    half = events // 2
    chunks = dsem.shape[0]
    cut = depth // chunks
    row, col = lax.axis_index("row"), lax.axis_index("col")
    me = row * cols + col
    side = lax.rem(col, 2)
    group = col // 2
    order = block_order(groups)
    width = 2 if PAIRED else 1
    steps = [order[i : i + width] for i in range(0, len(order), width)]
    sent_at = {block: n for n, step in enumerate(steps) for block in step}

    small = [
        pltpu.make_async_copy(src, dst, smallsem.at[i])
        for i, (src, dst) in enumerate(
            [
                (owner_hbm, flat), (site_hbm, site_ref), (class_hbm, class_ref), (value_hbm, value_ref),
                (curve_hbm, curve_ref), (inter_hbm, inter), (count_hbm, count_ref),
            ]
        )
    ]

    def group_at(g):
        return lax.rem(group + 1 + g, groups)

    def fetch(i):
        kind, g = order[i]
        target = group_at(g) * 2 + ((1 - side) if kind == "A" else side)
        start = pl.multiple_of(target * sites, 16)
        return pltpu.make_async_copy(
            factor.at[pl.ds(start, sites)], fbuf.at[pl.ds(i * sites, sites)], fsem.at[i]
        )

    def fetch_draws(j):
        part = pl.ds(j * cut, cut)
        return pltpu.make_async_copy(draws.at[part], dbuf.at[part], dsem.at[j])

    fetches = [functools.partial(fetch, i) for i in range(width)]
    fetches += [functools.partial(fetch_draws, j) for j in range(chunks)]
    fetches += [functools.partial(fetch, i) for i in range(width, len(order))]
    state = {"started": 0, "arrived": 0}

    def start_to(n):
        while state["started"] < min(n, len(fetches)):
            fetches[state["started"]]().start()
            state["started"] += 1

    def wait_to(n):
        while state["arrived"] < n:
            fetches[state["arrived"]]().wait()
            state["arrived"] += 1
            start_to(state["arrived"] + WINDOW)

    small[0].start()
    start_to(WINDOW)
    for copy in small[1:]:
        copy.start()

    barrier = pltpu.get_barrier_semaphore()

    @pl.loop(1, devices)
    def _(i):
        to = lax.rem(me + i, devices)
        pl.semaphore_signal(
            barrier, inc=1, device_id=(to // cols, lax.rem(to, cols)), device_id_type=MESH
        )

    small[0].wait()
    for d in range(devices):
        line, at = divmod(d * sites, 128)
        piece = flat[line : line + 1, at : min(at + sites, 128)]
        if at + sites > 128:
            piece = jnp.concatenate([piece, flat[line + 1 : line + 2, : at + sites - 128]], axis=1)
        owner[d : d + 1, :] = piece
    own = owner[pl.ds(me, 1), :]
    onehot = lax.broadcasted_iota(jnp.int32, (devices, sites), 0) == own
    onehot = onehot.astype(jnp.float32)
    before = jnp.dot(
        onehot.astype(jnp.bfloat16), earlier_mask(sites), preferred_element_type=jnp.float32
    )
    rank = jnp.sum(onehot * before, axis=0, keepdims=True).astype(jnp.int32)
    slot = lax.broadcasted_iota(jnp.int32, (devices * SLOT, sites), 0)
    placing[...] = (slot == own * SLOT + rank).astype(jnp.float32).astype(jnp.bfloat16)
    for copy in small[1:]:
        copy.wait()

    def send_side(g):
        return pltpu.make_async_remote_copy(
            src_ref=ysend.at[g], dst_ref=yrecv.at[g], send_sem=yssem.at[g], recv_sem=yrsem.at[g],
            device_id=(row, col + 1 - 2 * side), device_id_type=MESH,
        )

    def send_group(g):
        return pltpu.make_async_remote_copy(
            src_ref=zsend.at[g], dst_ref=zrecv.at[g], send_sem=zssem.at[g], recv_sem=zrsem.at[g],
            device_id=(row, group_at(g) * 2 + side), device_id_type=MESH,
        )

    lag = 2 if PAIRED else 4
    pending = []
    first = 0
    for n, step in enumerate(steps):
        count = len(step)
        lo, hi = first * sites, (first + count) * sites
        if n == 0:
            acc = jnp.zeros((count * sites, events), jnp.float32)
            for j in range(chunks):
                wait_to(count + j + 1)
                acc += jnp.dot(
                    fbuf[lo:hi, j * cut : (j + 1) * cut], dbuf[j * cut : (j + 1) * cut, :],
                    preferred_element_type=jnp.float32,
                )
            pl.semaphore_wait(barrier, devices - 1)
        else:
            wait_to(chunks + first + count)
            acc = jnp.dot(fbuf[lo:hi, :], dbuf[...], preferred_element_type=jnp.float32)
        for b, (kind, g) in enumerate(step):
            part = acc[b * sites : (b + 1) * sites]
            if kind == "A":
                ysend[g] = part.astype(jnp.bfloat16)
                send_side(g).start()
            else:
                held[g] = part
                if g < groups - 1:
                    pending.append(g)
        last = n == len(steps) - 1
        while pending and (last or n >= sent_at["A", pending[0]] + lag):
            g = pending.pop(0)
            send_side(g).wait_recv()
            zsend[g] = (held[g] + yrecv[g].astype(jnp.float32)).astype(jnp.bfloat16)
            send_group(g).start()
        first += count

    own_group = groups - 1
    send_side(own_group).wait_recv()
    total = held[own_group] + yrecv[own_group].astype(jnp.float32)
    for g in range(groups - 1):
        send_group(g).wait_recv()
        total = total + zrecv[g].astype(jnp.float32)
    res_ref[...] = total
    written = [pltpu.make_async_copy(res_ref, res_out, outsem.at[0])]
    written[0].start()
    motion = (median_log + intra_scale * total + inter[...]).astype(jnp.bfloat16)
    parts = [
        jnp.dot(placing[...], motion[:, h * half : (h + 1) * half], preferred_element_type=jnp.float32)
        .reshape(devices, SLOT, half)
        for h in range(2)
    ]
    outbuf[...] = jnp.concatenate(parts, axis=1).astype(jnp.bfloat16)

    @pl.loop(0, devices)
    def _(i):
        to_group = lax.rem(group + groups // 2 + i // (2 * rows), groups)
        to_row = lax.rem(row + (i // 2) % rows, rows)
        to_col = to_group * 2 + lax.rem(side + i, 2)
        to = to_row * cols + to_col

        @pl.when(to != me)
        def _():
            pltpu.make_async_remote_copy(
                src_ref=outbuf.at[to], dst_ref=inbuf.at[me], send_sem=ssem, recv_sem=rsem,
                device_id=(to_row, to_col), device_id_type=MESH,
            ).start()

    inbuf[me] = outbuf[me]
    prepare_assets(
        me, count_ref[0], owner, site_ref, class_ref, value_ref, curve_ref,
        select_ref, table_ref, agg_ref,
    )
    for g in range(groups):
        send_side(g).wait_send()
    for g in range(groups - 1):
        send_group(g).wait_send()
    others = pl.ds(0, devices - 1)
    pltpu.make_async_copy(inbuf.at[others], inbuf.at[others], rsem).wait()
    levels = curve_ref.shape[0]
    came = inbuf[...].astype(jnp.float32)
    for h in range(2):
        felt = came[:, h * SLOT : (h + 1) * SLOT, :].reshape(devices * SLOT, half)
        level = jnp.clip((felt - grid_low) * ((levels - 1) / grid_span), 0.0, levels - 1.0)
        below = jnp.minimum(level.astype(jnp.int32), levels - 2)
        floor = below.astype(jnp.float32)
        share = level - floor
        stage_ref[:, h * half : (h + 1) * half] = floor.astype(jnp.bfloat16)
        stage_ref[:, events + h * half : events + (h + 1) * half] = share.astype(jnp.bfloat16)
        loss = curve_at(agg_ref[...], below, share)
        regions[0, :, h * half : (h + 1) * half] = jnp.sum(loss.reshape(devices, 8, half), axis=0)
    copies = []
    for i in range(1, rows):
        copy = pltpu.make_async_remote_copy(
            src_ref=regions.at[0], dst_ref=regions.at[i], send_sem=gssem.at[i], recv_sem=grsem.at[i],
            device_id=(lax.rem(row + i, rows), col), device_id_type=MESH,
        )
        copy.start()
        copies.append(copy)
    assets = loss_ref.shape[0]
    for base in range(0, assets, TILE):
        at = slice(base, base + TILE)
        loss_ref[at, :] = tile_losses(select_ref[:, at], table_ref[at, :], stage_ref[...])
        part = pl.ds(base, TILE)
        copy = pltpu.make_async_copy(loss_ref.at[part], loss_out.at[part], outsem.at[2 + base // TILE])
        copy.start()
        written.append(copy)
    pltpu.make_async_copy(outbuf.at[others], outbuf.at[others], ssem).wait()
    total = regions[0]
    for i, copy in enumerate(copies):
        copy.wait_recv()
        total = total + regions[i + 1]
    scale = 1.0 / (assets * rows)
    region_ref[...] = jnp.sum(total, axis=0, keepdims=True) * scale
    copy = pltpu.make_async_copy(region_ref, region_out, outsem.at[1])
    copy.start()
    written.append(copy)
    for copy in copies:
        copy.wait_send()
    for copy in written:
        copy.wait()


def curve_at(table, below, share):
    low = jnp.take_along_axis(table[:, :128], below, axis=1, mode="promise_in_bounds")
    rise = jnp.take_along_axis(table[:, 128:], below, axis=1, mode="promise_in_bounds")
    return low + share * rise


def tile_losses(select, table, stage):
    felt = lax.dot_general(select, stage, (((0,), (0,)), ((), ())), preferred_element_type=jnp.float32)
    events = stage.shape[1] // 2
    parts = []
    for h in range(events // 128):
        below = felt[:, h * 128 : (h + 1) * 128].astype(jnp.int32)
        share = felt[:, events + h * 128 : events + (h + 1) * 128]
        parts.append(curve_at(table, below, share))
    return jnp.concatenate(parts, axis=1)


def prepare_assets(
    me, count, owner, site_ref, class_ref, value_ref, curve_ref, select_ref, table_ref, agg_ref,
):
    devices, sites = owner.shape
    slots = select_ref.shape[0]
    assets = site_ref.shape[1]
    levels, classes = curve_ref.shape
    wide = jnp.broadcast_to(owner[...][:, None, :], (devices, SLOT, sites)).reshape(slots, sites)
    mine = (wide == me).astype(jnp.float32)
    rank = jnp.dot(mine.astype(jnp.bfloat16), earlier_mask(sites), preferred_element_type=jnp.float32)
    slot = lax.broadcasted_iota(jnp.int32, (slots, sites), 0)
    wanted = lax.rem(slot, SLOT).astype(jnp.float32)
    number = (slot // SLOT) * sites + lax.broadcasted_iota(jnp.int32, (slots, sites), 1) + 1
    hit = jnp.where((mine > 0.0) & (rank == wanted), number, 0)
    mysite = jnp.sum(hit, axis=1, keepdims=True) - 1
    curve = curve_ref[...].astype(jnp.float32)
    blank = jnp.zeros((128 - levels, classes), jnp.float32)
    curve = jnp.concatenate([curve, blank, curve[1:], curve[levels - 1 :], blank], axis=0)
    curve = curve.astype(jnp.bfloat16)
    value = value_ref[...].astype(jnp.float32)
    agg = jnp.zeros((slots, 256), jnp.float32)
    for base in range(0, assets, TILE):
        at = slice(base, base + TILE)
        select = (mysite == site_ref[:, at]).astype(jnp.float32)
        owned = jnp.sum(select, axis=0, keepdims=True)
        select = select.astype(jnp.bfloat16)
        select_ref[:, at] = select
        place = base + lax.broadcasted_iota(jnp.int32, (1, TILE), 1)
        live = jnp.where(place < count, owned, 0.0)
        first = base // 128
        price = jnp.concatenate([value[first + i : first + i + 1] for i in range(TILE // 128)], axis=1)
        chosen = lax.broadcasted_iota(jnp.int32, (classes, TILE), 0) == class_ref[:, at]
        chosen = jnp.where(chosen, price * live, 0.0).astype(jnp.bfloat16)
        table = lax.dot_general(
            chosen, curve, (((0,), (1,)), ((), ())), preferred_element_type=jnp.float32
        )
        table = jnp.concatenate([table[:, :128], table[:, 128:] - table[:, :128]], axis=1)
        table_ref[at, :] = table
        agg = agg + jnp.dot(select, table.astype(jnp.bfloat16), preferred_element_type=jnp.float32)
    agg_ref[...] = agg


def write_kernel(parts, res_in, loss_in, region_in, res_out, loss_out, region_out, res, loss, region, came, sent):
    cut = loss.shape[0] // parts
    moves = [(res_in, res, res_out), (region_in, region, region_out)]
    for i in range(parts):
        part = pl.ds(i * cut, cut)
        moves.append((loss_in.at[part], loss.at[part], loss_out.at[part]))
    reads = [pltpu.make_async_copy(src, mid, came.at[i]) for i, (src, mid, _) in enumerate(moves)]
    writes = [pltpu.make_async_copy(mid, dst, sent.at[i]) for i, (_, mid, dst) in enumerate(moves)]
    for read in reads[::-1]:
        read.start()
    for read, write in zip(reads[::-1], writes[::-1]):
        read.wait()
        write.start()
    for write in writes:
        write.wait()


def body(
    rows, cols,
    factor_panel, normal_draws, inter_event, site_owner, asset_site, asset_class, asset_value, asset_count, damage_curve,
):
    devices = rows * cols
    groups = cols // 2
    local, depth = factor_panel.shape
    sites = local // cols
    events = normal_draws.shape[1]
    assets = asset_site.shape[0]
    slots = devices * SLOT
    chunks = 3
    hbm = pl.BlockSpec(memory_space=pltpu.HBM)
    dma = pltpu.SemaphoreType.DMA
    bf16, f32, i32 = jnp.bfloat16, jnp.float32, jnp.int32
    shapes = (
        jax.ShapeDtypeStruct((sites, events), f32),
        jax.ShapeDtypeStruct((assets, events), f32),
        jax.ShapeDtypeStruct((1, events), f32),
    )
    res, loss, region = pl.pallas_call(
        functools.partial(motion_kernel, rows, cols),
        out_shape=shapes,
        in_specs=[hbm] * 9,
        out_specs=(hbm,) * 3,
        scratch_shapes=[
            pltpu.VMEM((sites, events), f32),
            pltpu.VMEM((assets, events), f32),
            pltpu.VMEM((1, events), f32),
            pltpu.VMEM((slots, assets), bf16),
            pltpu.VMEM((assets, 256), f32),
            pltpu.VMEM((slots, 2 * events), bf16),
            pltpu.VMEM((local, depth), bf16),
            pltpu.VMEM((depth, events), bf16),
            pltpu.VMEM((groups, sites, events), bf16),
            pltpu.VMEM((groups, sites, events), bf16),
            pltpu.VMEM((groups, sites, events), f32),
            pltpu.VMEM((groups, sites, events), bf16),
            pltpu.VMEM((groups, sites, events), bf16),
            pltpu.VMEM((slots, sites), bf16),
            pltpu.VMEM((devices, 2 * SLOT, events // 2), bf16),
            pltpu.VMEM((devices, 2 * SLOT, events // 2), bf16),
            pltpu.VMEM((rows, 8, events), f32),
            pltpu.VMEM((slots, 256), f32),
            pltpu.VMEM((devices, sites), i32),
            pltpu.SMEM((1,), i32),
            pltpu.VMEM((1, events), f32),
            pltpu.VMEM((devices * sites // 128, 128), i32),
            pltpu.VMEM((1, assets), i32),
            pltpu.VMEM((1, assets), i32),
            pltpu.VMEM((assets // 128, 128), bf16),
            pltpu.VMEM(damage_curve.shape, bf16),
            dma((cols,)), dma((chunks,)), dma((groups,)), dma((groups,)), dma((groups,)), dma((groups,)),
            dma, dma, dma((rows,)), dma((rows,)), dma((7,)), dma((2 + assets // TILE,)),
        ],
        compiler_params=pltpu.CompilerParams(
            collective_id=0, has_side_effects=True, vmem_limit_bytes=K1 << 10
        ),
        name="everything",
    )(
        asset_count, factor_panel, normal_draws, inter_event.reshape(1, events), site_owner.reshape(devices * sites // 128, 128),
        asset_site.reshape(1, assets), asset_class.reshape(1, assets),
        asset_value.reshape(assets // 128, 128), damage_curve,
    )
    return pl.pallas_call(
        functools.partial(write_kernel, PARTS),
        out_shape=shapes,
        in_specs=[hbm] * 3,
        out_specs=(hbm,) * 3,
        scratch_shapes=[pltpu.VMEM(shape.shape, f32) for shape in shapes] + [dma((PARTS + 2,)), dma((PARTS + 2,))],
        compiler_params=pltpu.CompilerParams(vmem_limit_bytes=K2 << 20),
        name="writing",
    )(res, loss, region)


def solution(mesh):
    placed = (
        P("row", "col"),
        P("col", None),
        P(),
        P(),
        P(("row", "col")),
        P(("row", "col")),
        P(("row", "col")),
        P(("row", "col")),
        P(),
    )
    return jax.shard_map(
        functools.partial(body, mesh.shape["row"], mesh.shape["col"]),
        mesh=mesh,
        in_specs=placed,
        out_specs=(P(("row", "col"), None), P(("row", "col"), None), P("col", None)),
        check_vma=False,
    )
```

```python
import functools

import jax
import jax.numpy as jnp
from jax import lax
from jax.experimental import pallas as pl
from jax.experimental.pallas import tpu as pltpu
from jax.sharding import PartitionSpec as P

median_log = -1.0
intra_scale = 0.6
grid_low = -4.0
grid_span = 6.0
SLOT = 8
TILE = 256
K1 = 60 * 1024
K2 = 60
PARTS = 8
WINDOW = 16
PAIRED = True
MESH = pl.DeviceIdType.MESH


def block_order(groups):
    ahead = min(3, groups - 1)
    order = [("A", g) for g in range(ahead)]
    order.append(("B", 0))
    for g in range(ahead, groups):
        order += [("B", g - ahead + 1), ("A", g)]
    return order + [("B", g) for g in range(groups - ahead + 1, groups)]


def earlier_mask(size):
    i = lax.broadcasted_iota(jnp.int32, (size, size), 0)
    j = lax.broadcasted_iota(jnp.int32, (size, size), 1)
    return (i < j).astype(jnp.float32).astype(jnp.bfloat16)


def motion_kernel(
    rows, cols,
    count_hbm, factor, draws, inter_hbm, owner_hbm, site_hbm, class_hbm, value_hbm, curve_hbm,
    res_out, loss_out, region_out,
    res_ref, loss_ref, region_ref, select_ref, table_ref, stage_ref, fbuf, dbuf, ysend, yrecv, held, zsend, zrecv, placing, outbuf, inbuf, regions, agg_ref, owner,
    count_ref, inter, flat, site_ref, class_ref, value_ref, curve_ref,
    fsem, dsem, yssem, yrsem, zssem, zrsem, ssem, rsem, gssem, grsem, smallsem, outsem,
):
    devices = rows * cols
    groups = cols // 2
    sites, depth = factor.shape[0] // cols, factor.shape[1]
    events = draws.shape[1]
    half = events // 2
    chunks = dsem.shape[0]
    cut = depth // chunks
    row, col = lax.axis_index("row"), lax.axis_index("col")
    me = row * cols + col
    side = lax.rem(col, 2)
    group = col // 2
    order = block_order(groups)
    width = 2 if PAIRED else 1
    steps = [order[i : i + width] for i in range(0, len(order), width)]
    sent_at = {block: n for n, step in enumerate(steps) for block in step}

    small = [
        pltpu.make_async_copy(src, dst, smallsem.at[i])
        for i, (src, dst) in enumerate(
            [
                (owner_hbm, flat), (site_hbm, site_ref), (class_hbm, class_ref), (value_hbm, value_ref),
                (curve_hbm, curve_ref), (inter_hbm, inter), (count_hbm, count_ref),
            ]
        )
    ]

    def group_at(g):
        return lax.rem(group + 1 + g, groups)

    def fetch(i):
        kind, g = order[i]
        target = group_at(g) * 2 + ((1 - side) if kind == "A" else side)
        start = pl.multiple_of(target * sites, 16)
        return pltpu.make_async_copy(
            factor.at[pl.ds(start, sites)], fbuf.at[pl.ds(i * sites, sites)], fsem.at[i]
        )

    def fetch_draws(j):
        part = pl.ds(j * cut, cut)
        return pltpu.make_async_copy(draws.at[part], dbuf.at[part], dsem.at[j])

    fetches = [functools.partial(fetch, i) for i in range(width)]
    fetches += [functools.partial(fetch_draws, j) for j in range(chunks)]
    fetches += [functools.partial(fetch, i) for i in range(width, len(order))]
    state = {"started": 0, "arrived": 0}

    def start_to(n):
        while state["started"] < min(n, len(fetches)):
            fetches[state["started"]]().start(priority=int(state["started"] >= width + chunks))
            state["started"] += 1

    def wait_to(n):
        while state["arrived"] < n:
            fetches[state["arrived"]]().wait()
            state["arrived"] += 1
            start_to(state["arrived"] + WINDOW)

    small[0].start()
    start_to(WINDOW)
    for copy in small[1:]:
        copy.start()

    barrier = pltpu.get_barrier_semaphore()

    @pl.loop(1, devices)
    def _(i):
        to = lax.rem(me + i, devices)
        pl.semaphore_signal(
            barrier, inc=1, device_id=(to // cols, lax.rem(to, cols)), device_id_type=MESH
        )

    small[0].wait()
    for d in range(devices):
        line, at = divmod(d * sites, 128)
        piece = flat[line : line + 1, at : min(at + sites, 128)]
        if at + sites > 128:
            piece = jnp.concatenate([piece, flat[line + 1 : line + 2, : at + sites - 128]], axis=1)
        owner[d : d + 1, :] = piece
    own = owner[pl.ds(me, 1), :]
    onehot = lax.broadcasted_iota(jnp.int32, (devices, sites), 0) == own
    onehot = onehot.astype(jnp.float32)
    before = jnp.dot(
        onehot.astype(jnp.bfloat16), earlier_mask(sites), preferred_element_type=jnp.float32
    )
    rank = jnp.sum(onehot * before, axis=0, keepdims=True).astype(jnp.int32)
    slot = lax.broadcasted_iota(jnp.int32, (devices * SLOT, sites), 0)
    placing[...] = (slot == own * SLOT + rank).astype(jnp.float32).astype(jnp.bfloat16)
    for copy in small[1:]:
        copy.wait()

    def send_side(g):
        return pltpu.make_async_remote_copy(
            src_ref=ysend.at[g], dst_ref=yrecv.at[g], send_sem=yssem.at[g], recv_sem=yrsem.at[g],
            device_id=(row, col + 1 - 2 * side), device_id_type=MESH,
        )

    def send_group(g):
        return pltpu.make_async_remote_copy(
            src_ref=zsend.at[g], dst_ref=zrecv.at[g], send_sem=zssem.at[g], recv_sem=zrsem.at[g],
            device_id=(row, group_at(g) * 2 + side), device_id_type=MESH,
        )

    lag = 2 if PAIRED else 4
    pending = []
    first = 0
    for n, step in enumerate(steps):
        count = len(step)
        lo, hi = first * sites, (first + count) * sites
        if n == 0:
            acc = jnp.zeros((count * sites, events), jnp.float32)
            for j in range(chunks):
                wait_to(count + j + 1)
                acc += jnp.dot(
                    fbuf[lo:hi, j * cut : (j + 1) * cut], dbuf[j * cut : (j + 1) * cut, :],
                    preferred_element_type=jnp.float32,
                )
            pl.semaphore_wait(barrier, devices - 1)
        else:
            wait_to(chunks + first + count)
            acc = jnp.dot(fbuf[lo:hi, :], dbuf[...], preferred_element_type=jnp.float32)
        for b, (kind, g) in enumerate(step):
            part = acc[b * sites : (b + 1) * sites]
            if kind == "A":
                ysend[g] = part.astype(jnp.bfloat16)
                send_side(g).start()
            else:
                held[g] = part
                if g < groups - 1:
                    pending.append(g)
        last = n == len(steps) - 1
        while pending and (last or n >= sent_at["A", pending[0]] + lag):
            g = pending.pop(0)
            send_side(g).wait_recv()
            zsend[g] = (held[g] + yrecv[g].astype(jnp.float32)).astype(jnp.bfloat16)
            send_group(g).start()
        first += count

    own_group = groups - 1
    send_side(own_group).wait_recv()
    total = held[own_group] + yrecv[own_group].astype(jnp.float32)
    for g in range(groups - 1):
        send_group(g).wait_recv()
        total = total + zrecv[g].astype(jnp.float32)
    res_ref[...] = total
    written = [pltpu.make_async_copy(res_ref, res_out, outsem.at[0])]
    written[0].start()
    motion = (median_log + intra_scale * total + inter[...]).astype(jnp.bfloat16)
    parts = [
        jnp.dot(placing[...], motion[:, h * half : (h + 1) * half], preferred_element_type=jnp.float32)
        .reshape(devices, SLOT, half)
        for h in range(2)
    ]
    outbuf[...] = jnp.concatenate(parts, axis=1).astype(jnp.bfloat16)

    @pl.loop(1, devices)
    def _(i):
        to = lax.rem(me + i, devices)
        pltpu.make_async_remote_copy(
            src_ref=outbuf.at[to], dst_ref=inbuf.at[me], send_sem=ssem, recv_sem=rsem,
            device_id=(to // cols, lax.rem(to, cols)), device_id_type=MESH,
        ).start()

    inbuf[me] = outbuf[me]
    prepare_assets(
        me, count_ref[0], owner, site_ref, class_ref, value_ref, curve_ref,
        select_ref, table_ref, agg_ref,
    )
    for g in range(groups):
        send_side(g).wait_send()
    for g in range(groups - 1):
        send_group(g).wait_send()
    others = pl.ds(0, devices - 1)
    pltpu.make_async_copy(inbuf.at[others], inbuf.at[others], rsem).wait()
    levels = curve_ref.shape[0]
    came = inbuf[...].astype(jnp.float32)
    for h in range(2):
        felt = came[:, h * SLOT : (h + 1) * SLOT, :].reshape(devices * SLOT, half)
        level = jnp.clip((felt - grid_low) * ((levels - 1) / grid_span), 0.0, levels - 1.0)
        below = jnp.minimum(level.astype(jnp.int32), levels - 2)
        floor = below.astype(jnp.float32)
        share = level - floor
        stage_ref[:, h * half : (h + 1) * half] = floor.astype(jnp.bfloat16)
        stage_ref[:, events + h * half : events + (h + 1) * half] = share.astype(jnp.bfloat16)
        loss = curve_at(agg_ref[...], below, share)
        regions[0, :, h * half : (h + 1) * half] = jnp.sum(loss.reshape(devices, 8, half), axis=0)
    copies = []
    for i in range(1, rows):
        copy = pltpu.make_async_remote_copy(
            src_ref=regions.at[0], dst_ref=regions.at[i], send_sem=gssem.at[i], recv_sem=grsem.at[i],
            device_id=(lax.rem(row + i, rows), col), device_id_type=MESH,
        )
        copy.start()
        copies.append(copy)
    assets = loss_ref.shape[0]
    for base in range(0, assets, TILE):
        at = slice(base, base + TILE)
        loss_ref[at, :] = tile_losses(select_ref[:, at], table_ref[at, :], stage_ref[...])
        part = pl.ds(base, TILE)
        copy = pltpu.make_async_copy(loss_ref.at[part], loss_out.at[part], outsem.at[2 + base // TILE])
        copy.start()
        written.append(copy)
    pltpu.make_async_copy(outbuf.at[others], outbuf.at[others], ssem).wait()
    total = regions[0]
    for i, copy in enumerate(copies):
        copy.wait_recv()
        total = total + regions[i + 1]
    scale = 1.0 / (assets * rows)
    region_ref[...] = jnp.sum(total, axis=0, keepdims=True) * scale
    copy = pltpu.make_async_copy(region_ref, region_out, outsem.at[1])
    copy.start()
    written.append(copy)
    for copy in copies:
        copy.wait_send()
    for copy in written:
        copy.wait()


def curve_at(table, below, share):
    low = jnp.take_along_axis(table[:, :128], below, axis=1, mode="promise_in_bounds")
    rise = jnp.take_along_axis(table[:, 128:], below, axis=1, mode="promise_in_bounds")
    return low + share * rise


def tile_losses(select, table, stage):
    felt = lax.dot_general(select, stage, (((0,), (0,)), ((), ())), preferred_element_type=jnp.float32)
    events = stage.shape[1] // 2
    parts = []
    for h in range(events // 128):
        below = felt[:, h * 128 : (h + 1) * 128].astype(jnp.int32)
        share = felt[:, events + h * 128 : events + (h + 1) * 128]
        parts.append(curve_at(table, below, share))
    return jnp.concatenate(parts, axis=1)


def prepare_assets(
    me, count, owner, site_ref, class_ref, value_ref, curve_ref, select_ref, table_ref, agg_ref,
):
    devices, sites = owner.shape
    slots = select_ref.shape[0]
    assets = site_ref.shape[1]
    levels, classes = curve_ref.shape
    wide = jnp.broadcast_to(owner[...][:, None, :], (devices, SLOT, sites)).reshape(slots, sites)
    mine = (wide == me).astype(jnp.float32)
    rank = jnp.dot(mine.astype(jnp.bfloat16), earlier_mask(sites), preferred_element_type=jnp.float32)
    slot = lax.broadcasted_iota(jnp.int32, (slots, sites), 0)
    wanted = lax.rem(slot, SLOT).astype(jnp.float32)
    number = (slot // SLOT) * sites + lax.broadcasted_iota(jnp.int32, (slots, sites), 1) + 1
    hit = jnp.where((mine > 0.0) & (rank == wanted), number, 0)
    mysite = jnp.sum(hit, axis=1, keepdims=True) - 1
    curve = curve_ref[...].astype(jnp.float32)
    blank = jnp.zeros((128 - levels, classes), jnp.float32)
    curve = jnp.concatenate([curve, blank, curve[1:], curve[levels - 1 :], blank], axis=0)
    curve = curve.astype(jnp.bfloat16)
    value = value_ref[...].astype(jnp.float32)
    agg = jnp.zeros((slots, 256), jnp.float32)
    for base in range(0, assets, TILE):
        at = slice(base, base + TILE)
        select = (mysite == site_ref[:, at]).astype(jnp.float32)
        owned = jnp.sum(select, axis=0, keepdims=True)
        select = select.astype(jnp.bfloat16)
        select_ref[:, at] = select
        place = base + lax.broadcasted_iota(jnp.int32, (1, TILE), 1)
        live = jnp.where(place < count, owned, 0.0)
        first = base // 128
        price = jnp.concatenate([value[first + i : first + i + 1] for i in range(TILE // 128)], axis=1)
        chosen = lax.broadcasted_iota(jnp.int32, (classes, TILE), 0) == class_ref[:, at]
        chosen = jnp.where(chosen, price * live, 0.0).astype(jnp.bfloat16)
        table = lax.dot_general(
            chosen, curve, (((0,), (1,)), ((), ())), preferred_element_type=jnp.float32
        )
        table = jnp.concatenate([table[:, :128], table[:, 128:] - table[:, :128]], axis=1)
        table_ref[at, :] = table
        agg = agg + jnp.dot(select, table.astype(jnp.bfloat16), preferred_element_type=jnp.float32)
    agg_ref[...] = agg


def write_kernel(parts, res_in, loss_in, region_in, res_out, loss_out, region_out, res, loss, region, came, sent):
    cut = loss.shape[0] // parts
    moves = [(res_in, res, res_out), (region_in, region, region_out)]
    for i in range(parts):
        part = pl.ds(i * cut, cut)
        moves.append((loss_in.at[part], loss.at[part], loss_out.at[part]))
    reads = [pltpu.make_async_copy(src, mid, came.at[i]) for i, (src, mid, _) in enumerate(moves)]
    writes = [pltpu.make_async_copy(mid, dst, sent.at[i]) for i, (_, mid, dst) in enumerate(moves)]
    for read in reads[::-1]:
        read.start()
    for read, write in zip(reads[::-1], writes[::-1]):
        read.wait()
        write.start()
    for write in writes:
        write.wait()


def body(
    rows, cols,
    factor_panel, normal_draws, inter_event, site_owner, asset_site, asset_class, asset_value, asset_count, damage_curve,
):
    devices = rows * cols
    groups = cols // 2
    local, depth = factor_panel.shape
    sites = local // cols
    events = normal_draws.shape[1]
    assets = asset_site.shape[0]
    slots = devices * SLOT
    chunks = 3
    hbm = pl.BlockSpec(memory_space=pltpu.HBM)
    dma = pltpu.SemaphoreType.DMA
    bf16, f32, i32 = jnp.bfloat16, jnp.float32, jnp.int32
    shapes = (
        jax.ShapeDtypeStruct((sites, events), f32),
        jax.ShapeDtypeStruct((assets, events), f32),
        jax.ShapeDtypeStruct((1, events), f32),
    )
    res, loss, region = pl.pallas_call(
        functools.partial(motion_kernel, rows, cols),
        out_shape=shapes,
        in_specs=[hbm] * 9,
        out_specs=(hbm,) * 3,
        scratch_shapes=[
            pltpu.VMEM((sites, events), f32),
            pltpu.VMEM((assets, events), f32),
            pltpu.VMEM((1, events), f32),
            pltpu.VMEM((slots, assets), bf16),
            pltpu.VMEM((assets, 256), f32),
            pltpu.VMEM((slots, 2 * events), bf16),
            pltpu.VMEM((local, depth), bf16),
            pltpu.VMEM((depth, events), bf16),
            pltpu.VMEM((groups, sites, events), bf16),
            pltpu.VMEM((groups, sites, events), bf16),
            pltpu.VMEM((groups, sites, events), f32),
            pltpu.VMEM((groups, sites, events), bf16),
            pltpu.VMEM((groups, sites, events), bf16),
            pltpu.VMEM((slots, sites), bf16),
            pltpu.VMEM((devices, 2 * SLOT, events // 2), bf16),
            pltpu.VMEM((devices, 2 * SLOT, events // 2), bf16),
            pltpu.VMEM((rows, 8, events), f32),
            pltpu.VMEM((slots, 256), f32),
            pltpu.VMEM((devices, sites), i32),
            pltpu.SMEM((1,), i32),
            pltpu.VMEM((1, events), f32),
            pltpu.VMEM((devices * sites // 128, 128), i32),
            pltpu.VMEM((1, assets), i32),
            pltpu.VMEM((1, assets), i32),
            pltpu.VMEM((assets // 128, 128), bf16),
            pltpu.VMEM(damage_curve.shape, bf16),
            dma((cols,)), dma((chunks,)), dma((groups,)), dma((groups,)), dma((groups,)), dma((groups,)),
            dma, dma, dma((rows,)), dma((rows,)), dma((7,)), dma((2 + assets // TILE,)),
        ],
        compiler_params=pltpu.CompilerParams(
            collective_id=0, has_side_effects=True, vmem_limit_bytes=K1 << 10
        ),
        name="everything",
    )(
        asset_count, factor_panel, normal_draws, inter_event.reshape(1, events), site_owner.reshape(devices * sites // 128, 128),
        asset_site.reshape(1, assets), asset_class.reshape(1, assets),
        asset_value.reshape(assets // 128, 128), damage_curve,
    )
    return pl.pallas_call(
        functools.partial(write_kernel, PARTS),
        out_shape=shapes,
        in_specs=[hbm] * 3,
        out_specs=(hbm,) * 3,
        scratch_shapes=[pltpu.VMEM(shape.shape, f32) for shape in shapes] + [dma((PARTS + 2,)), dma((PARTS + 2,))],
        compiler_params=pltpu.CompilerParams(vmem_limit_bytes=K2 << 20),
        name="writing",
    )(res, loss, region)


def solution(mesh):
    placed = (
        P("row", "col"),
        P("col", None),
        P(),
        P(),
        P(("row", "col")),
        P(("row", "col")),
        P(("row", "col")),
        P(("row", "col")),
        P(),
    )
    return jax.shard_map(
        functools.partial(body, mesh.shape["row"], mesh.shape["col"]),
        mesh=mesh,
        in_specs=placed,
        out_specs=(P(("row", "col"), None), P(("row", "col"), None), P("col", None)),
        check_vma=False,
    )
```
